128 devices in a mesh: row: 16 (over x, z), grp: 8 (over y, core).
Axes of the slice: x: 4, y: 4, z: 4, core: 2. Of those that a mesh axis runs over, the one named last changes fastest.
Arguments:
- operator_tiles: bfloat16 [1024, 8, 256, 256], P(('row', 'grp')), may hold values from -0.125 to 0.125
- operator_columns: int32 [1024, 8], P(('row', 'grp')), may hold values from 0 to 1023, as said below
- operator_counts: int32 [1024], P(('row', 'grp')), may hold values from 2 to 8, as said below
- prolong_tiles: bfloat16 [1024, 3, 256, 128], P(('row', 'grp')), may hold values from -1.5 to 1.5
- prolong_columns: int32 [1024, 3], P(('row', 'grp')), may hold values from 0 to 255, as said below
- prolong_counts: int32 [1024], P(('row', 'grp')), may hold values from 1 to 3, as said below
Outputs:
- coarse_rows: float32 [256, 128, 1408], P(('row', 'grp'))
The draws below stay inside these ranges and needn't reach their ends.
Inputs may be any that keep to these rules, and one draw needn't show every extreme that they name: operator_columns[i, 0] = i; every entry lies within 4 panels of i; the live entries of a panel are distinct; entries at slots at or past operator_counts[i] are padding. `operator_counts`: some fine panel has all 8 tiles live. prolong_columns[i, 0] = i // 4; the entries of a panel are distinct and lie within 2 of i // 4. `prolong_counts`: some fine panel has all 3 tiles live.
All inputs are finite; a program needn't handle non-finite values.
Results may differ from the reference program's by a relative error of at most 0.0029.
Values may be sent and summed in bfloat16 or wider, within the bound.
No kernel may reach another device: no remote copies, remote signals or barrier semaphores. Data moves between devices by JAX's collectives and lax.ppermute only.
A program may use at most 128 MiB of HBM per device.

```python
import jax
import jax.numpy as jnp
from jax import lax

PANEL = 256
CPANEL = 128
RATIO = 4
REACH = 4
CREACH = 2
ATILES = 8
PTILES = 3
NFINE = 1024
NCOARSE = 256
FSPAN = 1
PFRAME = 5
QHALF = 3
BAND = 11


def draw_operator_columns(key, part):
    key = jax.random.fold_in(key, 11)
    span = 2 * REACH + 1
    offsets = jnp.arange(span, dtype=jnp.int32)[None, :] - REACH
    panel_ids = jnp.arange(NFINE, dtype=jnp.int32)[:, None]
    target = panel_ids + offsets
    valid = (target >= 0) & (target < NFINE)
    scores = jax.random.randint(key, (NFINE, span), 0, 2 ** 20) * 32 + jnp.arange(span, dtype=jnp.int32)[None, :]
    scores = scores + jnp.where(valid, 0, 2 ** 26)
    scores = jnp.where(offsets == 0, -1, scores)
    order = jnp.argsort(scores, axis=1)[:, :ATILES].astype(jnp.int32)
    return jnp.clip(panel_ids + order - REACH, 0, NFINE - 1).astype(jnp.int32)


def draw_operator_counts(key, part):
    key = jax.random.fold_in(key, 12)
    panel_ids = jnp.arange(NFINE, dtype=jnp.int32)
    valid_count = jnp.minimum(panel_ids, REACH) + jnp.minimum(NFINE - 1 - panel_ids, REACH) + 1
    values = jax.random.randint(key, (NFINE,), 2, ATILES + 1)
    values = jnp.minimum(values, valid_count)
    return values.at[REACH].set(ATILES).astype(jnp.int32)


def draw_prolong_columns(key, part):
    key = jax.random.fold_in(key, 13)
    span = 2 * CREACH + 1
    offsets = jnp.arange(span, dtype=jnp.int32)[None, :] - CREACH
    centre = (jnp.arange(NFINE, dtype=jnp.int32) // RATIO)[:, None]
    target = centre + offsets
    valid = (target >= 0) & (target < NCOARSE)
    scores = jax.random.randint(key, (NFINE, span), 0, 2 ** 20) * 32 + jnp.arange(span, dtype=jnp.int32)[None, :]
    scores = scores + jnp.where(valid, 0, 2 ** 26)
    scores = jnp.where(offsets == 0, -1, scores)
    order = jnp.argsort(scores, axis=1)[:, :PTILES].astype(jnp.int32)
    return (centre + order - CREACH).astype(jnp.int32)


def draw_prolong_counts(key, part):
    key = jax.random.fold_in(key, 14)
    values = jax.random.randint(key, (NFINE,), 1, PTILES + 1)
    return values.at[0].set(PTILES).astype(jnp.int32)


def shard_levels(stream_key, shape, shards, least, high):
    factor_of = 1.0
    for axis_at, shards_of in shards:
        draws = jax.random.uniform(jax.random.fold_in(jax.random.fold_in(stream_key, 6), axis_at), (shards_of,), jnp.float32, least / len(shards), high / len(shards))
        factor_of = factor_of * jnp.repeat(jnp.exp(draws), shape[axis_at] // shards_of).reshape((-1,) + (1,) * (len(shape) - 1 - axis_at))
    return factor_of


def gaussian(stream_key, shape, width, bound, cuts=(), kind=jnp.bfloat16):
    gain = shard_levels(stream_key, shape, cuts, -0.22, 0.18) if cuts else 1.0
    drawn = jax.random.normal(stream_key, shape, jnp.float32) * width * gain
    return jnp.minimum(jnp.maximum(drawn, -bound), bound).astype(kind)


def setup_inputs(seed: int = 0) -> dict:
    keys = jax.random.split(jax.random.key(seed), 7)
    return {
        "operator_tiles": gaussian(keys[0], (NFINE, ATILES, PANEL, PANEL), (PANEL * ATILES) ** -0.5, 0.125, ((0, 128),)),
        "operator_columns": draw_operator_columns(jax.random.fold_in(keys[6], 71), 0),
        "operator_counts": draw_operator_counts(jax.random.fold_in(keys[6], 71), 0),
        "prolong_tiles": gaussian(keys[3], (NFINE, PTILES, PANEL, CPANEL), 0.25, 1.5, ((0, 128),)),
        "prolong_columns": draw_prolong_columns(jax.random.fold_in(keys[6], 71), 0),
        "prolong_counts": draw_prolong_counts(jax.random.fold_in(keys[6], 71), 0),
    }


def make_slots(columns, counts, panel_ids):
    centre = panel_ids // RATIO
    slot_index = columns - centre[:, None] + CREACH
    live = jnp.arange(PTILES, dtype=jnp.int32)[None, :] < counts[:, None]
    return jnp.where(live, slot_index, -1).astype(jnp.int32)


def expand_frames(tiles, slots):
    select = (slots[:, :, None] == jnp.arange(PFRAME, dtype=jnp.int32)[None, None, :]).astype(jnp.float32)
    frame = jnp.einsum("nqs,nqpc->npsc", select, tiles.astype(jnp.float32))
    return frame.reshape(tiles.shape[0], tiles.shape[2], PFRAME * tiles.shape[3]).astype(jnp.bfloat16)


def reference(operator_tiles, operator_columns, operator_counts, prolong_tiles, prolong_columns, prolong_counts):
    panel_ids = jnp.arange(NFINE, dtype=jnp.int32)
    slots = make_slots(prolong_columns, prolong_counts, panel_ids)
    frames = expand_frames(prolong_tiles, slots)
    width_q = (2 * QHALF + 1) * CPANEL
    width_f = PFRAME * CPANEL

    def one_panel(index, result):
        index = jnp.asarray(index).astype(jnp.int32)
        centre = index // RATIO
        product = jnp.zeros((PANEL, width_q), jnp.float32)
        for slot_k in range(ATILES):
            target = operator_columns[index, slot_k].astype(jnp.int32)
            offset = ((target // RATIO - centre + FSPAN) * CPANEL).astype(jnp.int32)
            weight = (slot_k < operator_counts[index]).astype(jnp.float32)
            term = jnp.dot(operator_tiles[index, slot_k], frames[target], preferred_element_type=jnp.float32) * weight
            zero = jnp.zeros((), jnp.int32)
            current = lax.dynamic_slice(product, (zero, offset), (PANEL, width_f))
            product = lax.dynamic_update_slice(product, current + term, (zero, offset))
        rounded = product.astype(jnp.bfloat16)
        for slot_t in range(PTILES):
            target_row = prolong_columns[index, slot_t].astype(jnp.int32)
            shift_s = target_row - centre + CREACH
            weight = (slot_t < prolong_counts[index]).astype(jnp.float32)
            term = jnp.dot(prolong_tiles[index, slot_t].T, rounded, preferred_element_type=jnp.float32) * weight
            zero = jnp.zeros((), jnp.int32)
            start = ((2 * CREACH - shift_s) * CPANEL).astype(jnp.int32)
            current = lax.dynamic_slice(result, (target_row, zero, start), (1, CPANEL, width_q))
            result = lax.dynamic_update_slice(result, current + term[None], (target_row, zero, start))
        return result

    initial = jnp.zeros((NCOARSE, CPANEL, BAND * CPANEL), jnp.float32)
    return lax.fori_loop(0, NFINE, one_panel, initial)
```

```python
import jax
import jax.numpy as jnp
from jax import lax
from jax.experimental import pallas as pl
from jax.experimental.pallas import tpu as pltpu
from jax.sharding import PartitionSpec as P

AXES = ("row", "grp")
PANEL = 256
CP = 128
HALF = 4
SLOTS = 3
BAND = 11
DEAD = 7
PAY_ROWS = HALF * SLOTS * PANEL
META_ROWS = 16
VMEM_LIMIT = 48 * 1024 * 1024


def device_id():
    grp = lax.axis_index("grp")
    return lax.axis_index("row") * lax.axis_size("grp") + grp, lax.rem(grp, 2)


def slot_of(columns, counts, device, panel, slot):
    s = columns[panel, slot] - (2 * device + lax.div(panel, HALF)) + 2
    return jnp.where(slot < counts[panel], s, DEAD)


def tile_at(ref, index):
    return ref[pl.ds(pl.multiple_of(index * PANEL, PANEL), PANEL), :]


def three(ref, panel):
    return jnp.concatenate([tile_at(ref, panel * SLOTS + t) for t in range(SLOTS)], axis=1)


def dot(a, b):
    return jnp.dot(a, b, preferred_element_type=jnp.float32)


def dot_t(a, b):
    return lax.dot_general(a, b, (((0,), (0,)), ((), ())), preferred_element_type=jnp.float32)


def pack_kernel(columns, counts, tiles, on_ref, off_ref, meta, sems):
    device, parity = device_id()
    copies = []
    for at, (ref, half) in enumerate(((off_ref, parity), (on_ref, 1 - parity))):
        copies.append(
            pltpu.make_async_copy(
                tiles.at[pl.ds(pl.multiple_of(half * PAY_ROWS, PAY_ROWS), PAY_ROWS)],
                ref.at[pl.ds(0, PAY_ROWS)],
                sems.at[2 * at],
            )
        )
        copies[-1].start()
    lane = lax.broadcasted_iota(jnp.int32, (META_ROWS, CP), 1)
    for at, (ref, half) in enumerate(((off_ref, parity), (on_ref, 1 - parity))):
        values = jnp.zeros((META_ROWS, CP), jnp.int32)
        for p in range(HALF):
            for t in range(SLOTS):
                s = slot_of(columns, counts, device, half * HALF + p, t)
                values = jnp.where(lane == p * SLOTS + t, s, values)
        meta[at] = values.astype(jnp.float32).astype(jnp.bfloat16)
        copies.append(
            pltpu.make_async_copy(meta.at[at], ref.at[pl.ds(PAY_ROWS, META_ROWS)], sems.at[2 * at + 1])
        )
        copies[-1].start()
    for copy in copies:
        copy.wait()


def border_kernel(ocols, ocnt, pcols, pcnt, oper, tiles, out, abuf, px, acc, asem, psem):
    device, parity = device_id()

    def case(il, k):
        i = parity * HALF + il
        j = ocols[i, k] - 8 * device
        jo = jnp.where(parity == 1, j - 8, j + HALF)
        hit = (k < ocnt[i]) & (jo >= 0) & (jo < HALF)
        return i, jnp.clip(jo, 0, HALF - 1), hit

    p_copy = pltpu.make_async_copy(
        tiles.at[pl.ds(pl.multiple_of(parity * PAY_ROWS, PAY_ROWS), PAY_ROWS)], px, psem.at[0]
    )
    p_copy.start()

    def a_copy(il, k, i):
        return pltpu.make_async_copy(oper.at[i, k], abuf.at[il * 8 + k], asem.at[il * 8 + k])

    for il in range(HALF):
        for k in range(1, 8):
            i, _, hit = case(il, k)

            @pl.when(hit)
            def _():
                a_copy(il, k, i).start()

    acc[...] = jnp.zeros_like(acc)
    p_copy.wait()
    for il in range(HALF):
        i0 = parity * HALF + il
        rows = []
        for t in range(1, SLOTS):
            s = slot_of(pcols, pcnt, device, i0, t)
            r = parity + s - 2
            near = (parity == 1) & (r == 2) | (parity == 0) & (r == -1)
            far = (parity == 1) & (r == 3) | (parity == 0) & (r == -2)
            live = s < DEAD
            rows.append(jnp.where(live & near, 0, jnp.where(live & far, 1, 2)))
        for k in range(1, 8):
            i, jo, hit = case(il, k)

            @pl.when(hit)
            def _():
                a_copy(il, k, i).wait()
                lhs = jnp.concatenate([tile_at(px, il * SLOTS + 1), tile_at(px, il * SLOTS + 2)], axis=1)
                res = dot_t(lhs, abuf[il * 8 + k])
                for t in range(2):
                    acc[rows[t] * HALF + jo] += res[t * CP : (t + 1) * CP]

    for jo in range(HALF):
        for near in range(2):
            out[(jo * 2 + near) * CP : (jo * 2 + near + 1) * CP, :] = acc[near * HALF + jo].astype(jnp.bfloat16)


def local_kernel(
    ocols, ocnt, pcols, pcnt, oper, tiles, pay, roff, ron, own, abuf, px, prod, acc, meta_v, meta_s, slots, asem, psem
):
    device, parity = device_id()
    on = 1 - parity
    copies = [
        pltpu.make_async_copy(tiles, px.at[pl.ds(0, 2 * PAY_ROWS)], psem.at[0]),
        pltpu.make_async_copy(pay.at[pl.ds(0, PAY_ROWS)], px.at[pl.ds(2 * PAY_ROWS, PAY_ROWS)], psem.at[1]),
        pltpu.make_async_copy(pay.at[pl.ds(PAY_ROWS, META_ROWS)], meta_v.at[0], psem.at[2]),
    ]
    for copy in copies[::-1]:
        copy.start()

    def a_copy(i):
        return pltpu.make_async_copy(oper.at[i], abuf.at[i], asem.at[i])

    for i in range(8):
        a_copy(i).start()
    for i in range(8):
        for t in range(SLOTS):
            slots[i * SLOTS + t] = slot_of(pcols, pcnt, device, i, t)

    @pl.loop(0, 56)
    def _(n):
        acc[n] = jnp.zeros((CP, CP), jnp.float32)

    copies[2].wait()
    meta_i = meta_v[0].astype(jnp.float32).astype(jnp.int32)
    read_meta(meta_i, meta_s, slots, 8 * SLOTS)
    copies[0].wait()
    copies[1].wait()

    @pl.loop(0, 8)
    def _(i):
        m = lax.div(i, HALF)
        a_copy(i).wait()
        prod[...] = jnp.zeros_like(prod)

        def term(k):
            j = ocols[i, k] - 8 * device
            mine = (j >= 0) & (j < 8)
            jn = jnp.where(parity == 1, j + HALF, j - 8)
            theirs = (jn >= 0) & (jn < HALF)
            x = jnp.where(mine, j, jnp.where(theirs, 8 + jn, 0))
            live = (k < ocnt[i]) & (mine | theirs)
            base = lax.div(j + 8, HALF) - 2 - m + 1
            res = dot(abuf[i, k], three(px, x))
            for t in range(SLOTS):
                s = slots[x * SLOTS + t]
                q = jnp.where(live & (s < DEAD), base + s, 7)
                prod[q] += res[:, t * CP : (t + 1) * CP]

        for pair in range(4):
            if pair == 0:
                term(0)
                term(1)
            else:

                @pl.when(ocnt[i] > 2 * pair)
                def _(pair=pair):
                    term(2 * pair)
                    term(2 * pair + 1)

        rounded = jnp.concatenate([prod[q].astype(jnp.bfloat16) for q in range(7)], axis=1)
        for t in range(SLOTS):
            s = slots[i * SLOTS + t]
            row = jnp.where(s < DEAD, m + s, 6)
            res = dot_t(tile_at(px, i * SLOTS + t), rounded)
            for q in range(7):
                acc[row * 8 + m + q] += res[:, q * CP : (q + 1) * CP]

    near_off = jnp.where(parity == 1, 4, 1)
    far_off = jnp.where(parity == 1, 5, 0)
    for p in range(7):
        roff[p] = acc[near_off * 8 + p + on].astype(jnp.bfloat16)
    for p in range(6):
        roff[7 + p] = acc[far_off * 8 + p + 1].astype(jnp.bfloat16)
    near_on = jnp.where(parity == 1, 1, 4)
    far_on = jnp.where(parity == 1, 0, 5)
    for p in range(8):
        ron[p] = acc[near_on * 8 + p]
    for p in range(7):
        ron[8 + p] = acc[far_on * 8 + p + on]
    for r in range(2):
        for b in range(BAND):
            cb = b - 2 + r
            if 0 <= cb < 8:
                own[r * BAND + b] = acc[(r + 2) * 8 + cb]
            else:
                own[r * BAND + b] = jnp.zeros((CP, CP), jnp.float32)


def read_meta(values, meta_s, slots, at):
    vec, smem, sem = meta_s
    vec[...] = values[:8]
    copy = pltpu.make_async_copy(vec, smem, sem.at[0])
    copy.start()
    copy.wait()
    for l in range(HALF * SLOTS):
        slots[at + l] = smem[0, l]


def remote_kernel(
    ocols, ocnt, pcols, pcnt, oper, tiles, pay, bpay, own1, ron1, own, ron,
    abuf, px, prod, acc, meta_v, meta_s, slots, asem, psem,
):
    device, parity = device_id()
    copies = [
        pltpu.make_async_copy(
            tiles.at[pl.ds(pl.multiple_of(parity * PAY_ROWS, PAY_ROWS), PAY_ROWS)],
            px.at[pl.ds(0, PAY_ROWS)],
            psem.at[0],
        ),
        pltpu.make_async_copy(pay.at[pl.ds(0, PAY_ROWS)], px.at[pl.ds(PAY_ROWS, PAY_ROWS)], psem.at[1]),
        pltpu.make_async_copy(pay.at[pl.ds(PAY_ROWS, META_ROWS)], meta_v.at[0], psem.at[2]),
    ]
    for copy in copies[::-1]:
        copy.start()

    def case(il, k):
        i = parity * HALF + il
        j = ocols[i, k] - 8 * device
        jo = jnp.where(parity == 1, j - 8, j + HALF)
        hit = (k < ocnt[i]) & (jo >= 0) & (jo < HALF)
        return i, jnp.clip(jo, 0, HALF - 1), hit

    def a_copy(il, k, i):
        return pltpu.make_async_copy(oper.at[i, k], abuf.at[il * 8 + k], asem.at[il * 8 + k])

    for il in range(HALF):
        for k in range(1, 8):
            i, _, hit = case(il, k)

            @pl.when(hit)
            def _():
                a_copy(il, k, i).start()

    for il in range(HALF):
        for t in range(SLOTS):
            slots[il * SLOTS + t] = slot_of(pcols, pcnt, device, parity * HALF + il, t)

    for n in range(22):
        acc[n] = own1[n]
    for n in range(22, 32):
        acc[n] = jnp.zeros((CP, CP), jnp.float32)
    for p in range(8):
        acc[(1 - parity) * BAND + p + 3 * (1 - parity)] += ron1[p]
    for p in range(7):
        acc[parity * BAND + p + 4 * (1 - parity)] += ron1[8 + p]

    copies[2].wait()
    meta_i = meta_v[0].astype(jnp.float32).astype(jnp.int32)
    read_meta(meta_i, meta_s, slots, HALF * SLOTS)
    copies[0].wait()
    copies[1].wait()

    for il in range(HALF):
        res = dot(bpay[il * 2 * CP : (il + 1) * 2 * CP, :], three(px, il))
        for near in range(2):
            r = parity if near == 0 else 1 - parity
            for t in range(SLOTS):
                s = slots[il * SLOTS + t]
                at = jnp.where(s < DEAD, r * BAND + parity + s + 3 - r, 27)
                acc[at] += res[near * CP : (near + 1) * CP, t * CP : (t + 1) * CP]

    on_row = jnp.where(parity == 1, -1, 2)
    shift = jnp.where(parity == 1, 5, 2)
    for il in range(HALF):
        prod[...] = jnp.zeros_like(prod)
        for k in range(1, 8):
            i, jo, hit = case(il, k)

            @pl.when(hit)
            def _():
                a_copy(il, k, i).wait()
                res = dot(abuf[il * 8 + k], three(px, HALF + jo))
                for t in range(SLOTS):
                    s = slots[(HALF + jo) * SLOTS + t]
                    q = jnp.where(s < DEAD, s, 5)
                    prod[q] += res[:, t * CP : (t + 1) * CP]

        rounded = jnp.concatenate([prod[q].astype(jnp.bfloat16) for q in range(5)], axis=1)
        for t in range(SLOTS):
            s = slots[il * SLOTS + t]
            r = parity + s - 2
            mine = (r >= 0) & (r < 2)
            base = jnp.where(mine, r * BAND + shift - r, jnp.where(r == on_row, 22, 27))
            base = jnp.where(s < DEAD, base, 27)
            res = dot_t(tile_at(px, il * SLOTS + t), rounded)
            for q in range(5):
                acc[base + q] += res[:, q * CP : (q + 1) * CP]

    for n in range(22):
        own[n] = acc[n]
    for n in range(5):
        ron[n] = acc[22 + n]


def final_kernel(own, roff, ron, out):
    _, parity = device_id()
    for r in range(2):
        for b in range(BAND):
            out[r, :, b * CP : (b + 1) * CP] = own[r * BAND + b]

    def add(r, b, value):
        cols = pl.ds(pl.multiple_of(b * CP, CP), CP)
        out[r, :, cols] += value

    for p in range(7):
        add(parity, p + 4 * parity, roff[p].astype(jnp.float32))
    for p in range(6):
        add(1 - parity, p + 5 * parity, roff[7 + p].astype(jnp.float32))
    for p in range(5):
        add(1 - parity, p + 6 * (1 - parity), ron[p])


ANY = pl.BlockSpec(memory_space=pl.ANY)
VMEM = pl.BlockSpec(memory_space=pltpu.VMEM)
SMEM = pl.BlockSpec(memory_space=pltpu.SMEM)


def call(kernel, in_specs, out_specs, out_shape, scratch, flops, moved):
    return pl.pallas_call(
        kernel,
        in_specs=in_specs,
        out_specs=out_specs,
        out_shape=out_shape,
        scratch_shapes=scratch,
        compiler_params=pltpu.CompilerParams(vmem_limit_bytes=VMEM_LIMIT),
        cost_estimate=pl.CostEstimate(flops=flops, bytes_accessed=moved, transcendentals=0),
    )


def shape(dims, dtype=jnp.float32):
    return jax.ShapeDtypeStruct(dims, dtype)


def meta_scratch():
    return (pltpu.VMEM((8, CP), jnp.int32), pltpu.SMEM((8, CP), jnp.int32), pltpu.SemaphoreType.DMA((1,)))


def on_device(oper, ocols, ocnt, ptiles, pcols, pcnt):
    size = lax.axis_size(AXES)
    on_pairs = [(i, i ^ 1) for i in range(size)]
    off_pairs = [(i, i + 1) for i in range(1, size - 1, 2)]
    off_pairs += [(j, i) for i, j in off_pairs]
    tiles = ptiles.reshape(2 * PAY_ROWS, CP)
    bf16 = jnp.bfloat16
    dma = pltpu.SemaphoreType.DMA

    pay_on, pay_off = call(
        pack_kernel,
        [SMEM, SMEM, ANY],
        [ANY, ANY],
        [shape((PAY_ROWS + META_ROWS, CP), bf16)] * 2,
        [pltpu.VMEM((2, META_ROWS, CP), bf16), dma((4,))],
        0,
        4 * PAY_ROWS * CP * 2,
    )(pcols, pcnt, tiles)
    got_on = lax.ppermute(pay_on, AXES, on_pairs)
    got_off = lax.ppermute(pay_off, AXES, off_pairs)

    border = call(
        border_kernel,
        [SMEM] * 4 + [ANY, ANY],
        VMEM,
        shape((8 * CP, PANEL), bf16),
        [
            pltpu.VMEM((32, PANEL, PANEL), bf16),
            pltpu.VMEM((PAY_ROWS, CP), bf16),
            pltpu.VMEM((3 * HALF, CP, PANEL), jnp.float32),
            dma((32,)),
            dma((1,)),
        ],
        10 * 2 * PANEL**3,
        2**21,
    )(ocols, ocnt, pcols, pcnt, oper, tiles)
    got_border = lax.ppermute(border, AXES, off_pairs)

    roff, ron1, own1 = call(
        local_kernel,
        [SMEM] * 4 + [ANY, ANY, ANY],
        [VMEM] * 3,
        [shape((13, CP, CP), bf16), shape((15, CP, CP)), shape((22, CP, CP))],
        [
            pltpu.VMEM((8, 8, PANEL, PANEL), bf16),
            pltpu.VMEM((3 * PAY_ROWS, CP), bf16),
            pltpu.VMEM((8, PANEL, CP), jnp.float32),
            pltpu.VMEM((56, CP, CP), jnp.float32),
            pltpu.VMEM((1, META_ROWS, CP), bf16),
            meta_scratch(),
            pltpu.SMEM((64,), jnp.int32),
            dma((8,)),
            dma((3,)),
        ],
        5 * 10**9,
        2**24,
    )(ocols, ocnt, pcols, pcnt, oper, tiles, got_on)
    got_roff = lax.ppermute(roff, AXES, off_pairs)
    got_ron1 = lax.ppermute(ron1, AXES, on_pairs)

    own2, ron2 = call(
        remote_kernel,
        [SMEM] * 4 + [ANY, ANY, ANY, VMEM, VMEM, VMEM],
        [VMEM] * 2,
        [shape((22, CP, CP)), shape((5, CP, CP))],
        [
            pltpu.VMEM((32, PANEL, PANEL), bf16),
            pltpu.VMEM((2 * PAY_ROWS, CP), bf16),
            pltpu.VMEM((6, PANEL, CP), jnp.float32),
            pltpu.VMEM((32, CP, CP), jnp.float32),
            pltpu.VMEM((1, META_ROWS, CP), bf16),
            meta_scratch(),
            pltpu.SMEM((64,), jnp.int32),
            dma((32,)),
            dma((3,)),
        ],
        2 * 10**9,
        2**23,
    )(ocols, ocnt, pcols, pcnt, oper, tiles, got_off, got_border, own1, got_ron1)
    got_ron2 = lax.ppermute(ron2, AXES, on_pairs)

    return call(
        final_kernel,
        [VMEM] * 3,
        VMEM,
        shape((2, CP, BAND * CP)),
        [],
        10**6,
        2**22,
    )(own2, got_roff, got_ron2)


def solution(mesh):
    placed = (
        P(AXES, None, None, None),
        P(AXES, None),
        P(AXES),
        P(AXES, None, None, None),
        P(AXES, None),
        P(AXES),
    )
    return jax.shard_map(
        on_device, mesh=mesh, in_specs=placed, out_specs=P(AXES, None, None), check_vma=False
    )
```

```python
import jax
import jax.numpy as jnp
from jax import lax
from jax.experimental import pallas as pl
from jax.experimental.pallas import tpu as pltpu
from jax.sharding import PartitionSpec as P

AXES = ("row", "grp")
PANEL = 256
CP = 128
HALF = 4
SLOTS = 3
BAND = 11
DEAD = 7
TILE3 = SLOTS * CP
PAY = HALF * TILE3
META = 16
VMEM_LIMIT = 48 * 1024 * 1024
UNROLL = 12
F32 = jnp.float32
BF16 = jnp.bfloat16


def device_id():
    grp = lax.axis_index("grp")
    return lax.axis_index("row") * lax.axis_size("grp") + grp, lax.rem(grp, 2)


def slot_of(columns, counts, device, panel, slot):
    s = columns[slot, panel] - (2 * device + lax.div(panel, HALF)) + 2
    return jnp.where(slot < counts[panel], s, DEAD)


def rows_at(ref, start, size, step=CP):
    return ref[pl.ds(pl.multiple_of(start, step), size), :]


def dot(a, b):
    return jnp.dot(a, b, preferred_element_type=F32)


def dot_nt(a, b):
    return lax.dot_general(a, b, (((1,), (1,)), ((), ())), preferred_element_type=F32)


def off_hits(ocols, ocnt, device, parity, hits):
    found = 0
    for il in range(HALF):
        i = parity * HALF + il
        for k in range(1, 8):
            j = ocols[i, k] - 8 * device
            jo = jnp.where(parity == 1, j - 8, j + HALF)
            hits[found] = il * 64 + k * 8 + jo
            found += ((k < ocnt[i]) & (jo >= 0) & (jo < HALF)).astype(jnp.int32)
    return found


def field(code, shift, bits):
    return (code >> shift) & (2**bits - 1)


def clear(ref, count):
    @pl.loop(0, count)
    def _(n):
        ref[n] = jnp.zeros(ref.shape[1:], F32)


def first_kernel(
    ocols_h, ocnt_h, pcols_h, pcnt_h, oper, tiles, pt, on_ref, off_ref, abuf,
    raw, ocols, ocnt, pcols, pcnt, acc, hits, sems, asem,
):
    device, parity = device_id()
    halves = ((off_ref, parity), (on_ref, 1 - parity))
    copies = [
        pltpu.make_async_copy(tiles.at[pl.ds(half * HALF * SLOTS, HALF * SLOTS)], raw.at[at], sems.at[at])
        for at, (_, half) in enumerate(halves)
    ]
    small = [
        pltpu.make_async_copy(src, dst, sems.at[2 + at])
        for at, (src, dst) in enumerate(((ocols_h, ocols), (ocnt_h, ocnt), (pcols_h, pcols), (pcnt_h, pcnt)))
    ]
    for copy in small + copies:
        copy.start()
    for copy in small:
        copy.wait()
    count = off_hits(ocols, ocnt, device, parity, hits)

    def a_copy(n):
        code = hits[n]
        return pltpu.make_async_copy(
            oper.at[parity * HALF + field(code, 6, 2), field(code, 3, 3)], abuf.at[n], asem.at[n]
        )

    @pl.loop(0, count)
    def _(n):
        a_copy(n).start()

    lane = lax.broadcasted_iota(jnp.int32, (META, PANEL), 1)
    for ref, half in halves:
        values = jnp.zeros((META, PANEL), jnp.int32)
        for p in range(HALF):
            for t in range(SLOTS):
                s = slot_of(pcols, pcnt, device, half * HALF + p, t)
                values = jnp.where(lane == p * SLOTS + t, s, values)
        ref[PAY : PAY + META, :] = values.astype(F32).astype(BF16)
    for n in range(2 * HALF):
        acc[n] = jnp.zeros((CP, PANEL), F32)
    for at, (ref, half) in enumerate(halves):
        copies[at].wait()
        for n in range(HALF * SLOTS):
            turned = raw[at, n].T
            ref[n * CP : (n + 1) * CP, :] = turned
            pt[pl.ds(pl.multiple_of(half * PAY + n * CP, CP), CP), :] = turned

    @pl.loop(0, count)
    def _(n):
        a_copy(n).wait()

    @pl.loop(0, lax.div(count + 3, 4))
    def _(block):
        for u in range(4):
            n = block * 4 + u
            code = hits[n]
            il, jo = field(code, 6, 2), field(code, 0, 2)
            res = dot(rows_at(off_ref, (il * SLOTS + 1) * CP, 2 * CP), abuf[n])
            for t in range(1, SLOTS):
                s = slot_of(pcols, pcnt, device, parity * HALF + il, t)
                near = s == jnp.where(parity == 1, 3, 1)
                far = s == jnp.where(parity == 1, 4, 0)
                at = jnp.where(near, jo * 2, jnp.where(far, jo * 2 + 1, 8))
                acc[jnp.where(n < count, at, 8)] += res[(t - 1) * CP : t * CP]

    for n in range(2 * HALF):
        off_ref[PAY + META + n * CP : PAY + META + (n + 1) * CP, :] = acc[n].astype(BF16)


def read_meta(pay, vec, smem, sem, slots, at):
    vec[...] = pay[PAY : PAY + META, :].astype(F32).astype(jnp.int32)
    copy = pltpu.make_async_copy(vec, smem, sem)
    copy.start()
    copy.wait()
    for n in range(HALF * SLOTS):
        slots[at + n] = smem[0, n]


def local_kernel(
    ocols, ocnt, pcols, pcnt, oper, pt, pay, roff, ron, own,
    abuf, px, prod, acc, vec, smem, slots, hits, asem, psem,
):
    device, parity = device_id()
    on = 1 - parity
    copies = [
        pltpu.make_async_copy(pt, px.at[pl.ds(0, 2 * PAY)], psem.at[0]),
        pltpu.make_async_copy(pay.at[pl.ds(0, PAY)], px.at[pl.ds(2 * PAY, PAY)], psem.at[1]),
    ]
    for copy in copies:
        copy.start()

    def a_copy(n):
        code = hits[n]
        return pltpu.make_async_copy(oper.at[field(code, 9, 3), field(code, 6, 3)], abuf.at[n], asem.at[n])

    count = 0
    for i in range(8):
        began = count
        for k in range(8):
            j = ocols[i, k] - 8 * device
            mine = (j >= 0) & (j < 8)
            jn = jnp.where(parity == 1, j + HALF, j - 8)
            theirs = (jn >= 0) & (jn < HALF)
            x = jnp.where(mine, j, 8 + jn)
            base = ((j + 8) >> 2) - 1 - i // HALF
            hits[count] = i * 512 + k * 64 + x * 4 + base
            count += ((k < ocnt[i]) & (mine | theirs)).astype(jnp.int32)

        @pl.loop(began, count)
        def _(n):
            a_copy(n).start()

    for i in range(8):
        for t in range(SLOTS):
            slots[i * SLOTS + t] = slot_of(pcols, pcnt, device, i, t)
    read_meta(pay, vec, smem, psem.at[2], slots, 8 * SLOTS)
    clear(prod, 64)
    clear(acc, 48)
    for copy in copies:
        copy.wait()

    @pl.loop(0, count)
    def _(n):
        a_copy(n).wait()

    @pl.loop(0, lax.div(count + UNROLL - 1, UNROLL))
    def _(block):
        for u in range(UNROLL):
            n = jnp.minimum(block * UNROLL + u, count - 1)
            code = hits[n]
            i, x, base = field(code, 9, 3), field(code, 2, 4), field(code, 0, 2)
            base = jnp.where(block * UNROLL + u < count, i * 8 + base, 64)
            res = dot_nt(rows_at(px, x * TILE3, TILE3), abuf[n])
            for t in range(SLOTS):
                s = slots[x * SLOTS + t]
                prod[jnp.where(s < DEAD, base + s, 64)] += res[t * CP : (t + 1) * CP]

    @pl.loop(0, 2)
    def _(m):
        for p in range(HALF):
            i = m * HALF + p
            lhs = rows_at(px, i * TILE3, TILE3)
            at = []
            for t in range(SLOTS):
                s = slots[i * SLOTS + t]
                at.append(jnp.where(s < DEAD, m + s, 6) * 8 + m)
            for q0 in range(0, 7, 2):
                wide = min(2, 7 - q0)
                rhs = jnp.concatenate([prod[i * 8 + q0 + w].astype(BF16) for w in range(wide)], axis=0)
                res = dot_nt(lhs, rhs)
                for t in range(SLOTS):
                    for w in range(wide):
                        acc[at[t] + q0 + w] += res[t * CP : (t + 1) * CP, w * CP : (w + 1) * CP]

    near_off = jnp.where(parity == 1, 4, 1)
    far_off = jnp.where(parity == 1, 5, 0)
    for p in range(7):
        roff[p] = acc[near_off * 8 + p + on].astype(BF16)
    for p in range(6):
        roff[7 + p] = acc[far_off * 8 + p + 1].astype(BF16)
    near_on = jnp.where(parity == 1, 1, 4)
    far_on = jnp.where(parity == 1, 0, 5)
    for p in range(8):
        ron[p] = acc[near_on * 8 + p].astype(BF16)
    for p in range(7):
        ron[8 + p] = acc[far_on * 8 + p + on].astype(BF16)
    for r in range(2):
        for b in range(BAND):
            cb = b - 2 + r
            if 0 <= cb < 8:
                own[r * BAND + b] = acc[(r + 2) * 8 + cb]
            else:
                own[r * BAND + b] = jnp.zeros((CP, CP), F32)


def merge_kernel(own1, ron1, own):
    _, parity = device_id()
    on = 1 - parity
    for n in range(22):
        own[n] = own1[n]
    for p in range(8):
        own[on * BAND + p + 3 * on] += ron1[p].astype(F32)
    for p in range(7):
        own[parity * BAND + p + 4 * on] += ron1[8 + p].astype(F32)


def remote_kernel(
    ocols, ocnt, pcols, pcnt, abuf, pt, pay, own1, own, ron, prod, acc, vec, smem, slots, hits, psem
):
    device, parity = device_id()
    vec[...] = pay[PAY : PAY + META, :].astype(F32).astype(jnp.int32)
    meta = pltpu.make_async_copy(vec, smem, psem.at[0])
    meta.start()
    count = off_hits(ocols, ocnt, device, parity, hits)
    for il in range(HALF):
        for t in range(SLOTS):
            slots[il * SLOTS + t] = slot_of(pcols, pcnt, device, parity * HALF + il, t)
    clear(prod, HALF * 6)
    for n in range(22):
        acc[n] = own1[n]
    for n in range(22, 27):
        acc[n] = jnp.zeros((CP, CP), F32)
    meta.wait()

    @pl.loop(0, lax.div(count + 3, 4))
    def _(block):
        for u in range(4):
            n = jnp.minimum(block * 4 + u, count - 1)
            code = hits[n]
            il, jo = field(code, 6, 2), field(code, 0, 2)
            res = dot_nt(rows_at(pay, jo * TILE3, TILE3), abuf[n])
            for t in range(SLOTS):
                s = smem[0, jo * SLOTS + t]
                live = (s < DEAD) & (block * 4 + u < count)
                prod[jnp.where(live, il * 6 + s, 5)] += res[t * CP : (t + 1) * CP]

    on_row = jnp.where(parity == 1, -1, 2)
    shift = jnp.where(parity == 1, 5, 2)
    for il in range(HALF):
        lhs = rows_at(pt, (parity * HALF + il) * TILE3, TILE3)
        b_at = PAY + META + il * 2 * CP
        b_res = dot_nt(pay[b_at : b_at + 2 * CP, :], lhs)
        at = []
        for t in range(SLOTS):
            s = slots[il * SLOTS + t]
            r = parity + s - 2
            mine = (r >= 0) & (r < 2)
            base = jnp.where(mine, r * BAND + shift - r, jnp.where(r == on_row, 22, 27))
            at.append(jnp.where(s < DEAD, base, 27))
            for near in range(2):
                r = parity if near == 0 else 1 - parity
                b_row = jnp.where(s < DEAD, r * BAND + parity + s + 3 - r, 27)
                acc[b_row] += b_res[near * CP : (near + 1) * CP, t * CP : (t + 1) * CP]
        for q0 in range(0, 5, 2):
            wide = min(2, 5 - q0)
            rhs = jnp.concatenate([prod[il * 6 + q0 + w].astype(BF16) for w in range(wide)], axis=0)
            res = dot_nt(lhs, rhs)
            for t in range(SLOTS):
                for w in range(wide):
                    acc[at[t] + q0 + w] += res[t * CP : (t + 1) * CP, w * CP : (w + 1) * CP]

    for n in range(22):
        own[n] = acc[n]
    for n in range(5):
        ron[n] = acc[22 + n]


def final_kernel(own, roff, ron, out):
    _, parity = device_id()
    on = 1 - parity
    for r in range(2):
        for b in range(BAND):
            out[r, :, b * CP : (b + 1) * CP] = own[r * BAND + b]

    def add(r, b, value):
        cols = pl.ds(pl.multiple_of(b * CP, CP), CP)
        out[r, :, cols] += value

    for p in range(7):
        add(parity, p + 4 * parity, roff[p].astype(F32))
    for p in range(6):
        add(on, p + 5 * parity, roff[7 + p].astype(F32))
    for p in range(5):
        add(on, p + 6 * on, ron[p])


ANY = pl.BlockSpec(memory_space=pl.ANY)
HBM = pl.BlockSpec(memory_space=pltpu.HBM)
VMEM = pl.BlockSpec(memory_space=pltpu.VMEM)
SMEM = pl.BlockSpec(memory_space=pltpu.SMEM)


def call(kernel, in_specs, out_specs, out_shape, scratch):
    return pl.pallas_call(
        kernel,
        in_specs=in_specs,
        out_specs=out_specs,
        out_shape=out_shape,
        scratch_shapes=scratch,
        compiler_params=pltpu.CompilerParams(vmem_limit_bytes=VMEM_LIMIT),
        cost_estimate=pl.CostEstimate(flops=1000, bytes_accessed=1000, transcendentals=0),
    )


def shape(dims, dtype=F32):
    return jax.ShapeDtypeStruct(dims, dtype)


def on_device(oper, ocols, ocnt, ptiles, pcols, pcnt):
    size = lax.axis_size(AXES)
    on_pairs = [(i, i ^ 1) for i in range(size)]
    off_pairs = [(i, i + 1) for i in range(1, size - 1, 2)]
    off_pairs += [(j, i) for i, j in off_pairs]
    tiles = ptiles.reshape(8 * SLOTS, PANEL, CP)
    pcols = pcols.T
    dma = pltpu.SemaphoreType.DMA
    i32 = jnp.int32
    meta = [pltpu.VMEM((META, PANEL), i32), pltpu.SMEM((META, PANEL), i32), pltpu.SMEM((64,), i32)]

    pt, pay_on, pay_off, edge = call(
        first_kernel,
        [HBM] * 6,
        [VMEM] * 4,
        [
            shape((2 * PAY, PANEL), BF16),
            shape((PAY + META, PANEL), BF16),
            shape((PAY + META + 8 * CP, PANEL), BF16),
            shape((12, PANEL, PANEL), BF16),
        ],
        [
            pltpu.VMEM((2, HALF * SLOTS, PANEL, CP), BF16),
            pltpu.SMEM((8, 8), i32),
            pltpu.SMEM((8,), i32),
            pltpu.SMEM((SLOTS, 8), i32),
            pltpu.SMEM((8,), i32),
            pltpu.VMEM((9, CP, PANEL), F32),
            pltpu.SMEM((32,), i32),
            dma((6,)),
            dma((12,)),
        ],
    )(ocols, ocnt, pcols, pcnt, oper, tiles)
    got_on = lax.ppermute(pay_on, AXES, on_pairs)
    got_off = lax.ppermute(pay_off, AXES, off_pairs)

    roff, ron1, own1 = call(
        local_kernel,
        [SMEM] * 4 + [HBM, VMEM, VMEM],
        [VMEM] * 3,
        [shape((13, CP, CP), BF16), shape((15, CP, CP), BF16), shape((22, CP, CP))],
        [
            pltpu.VMEM((64, PANEL, PANEL), BF16),
            pltpu.VMEM((3 * PAY, PANEL), BF16),
            pltpu.VMEM((65 + 7, CP, PANEL), F32),
            pltpu.VMEM((56, CP, CP), F32),
            *meta,
            pltpu.SMEM((72,), i32),
            dma((64,)),
            dma((3,)),
        ],
    )(ocols, ocnt, pcols, pcnt, oper, pt, got_on)
    got_roff = lax.ppermute(roff, AXES, off_pairs)
    got_ron1 = lax.ppermute(ron1, AXES, on_pairs)
    own1 = call(merge_kernel, [VMEM] * 2, VMEM, shape((22, CP, CP)), [])(own1, got_ron1)

    own2, ron2 = call(
        remote_kernel,
        [SMEM] * 4 + [VMEM] * 4,
        [VMEM] * 2,
        [shape((22, CP, CP)), shape((5, CP, CP))],
        [
            pltpu.VMEM((HALF * 6, CP, PANEL), F32),
            pltpu.VMEM((32, CP, CP), F32),
            *meta,
            pltpu.SMEM((32,), i32),
            dma((1,)),
        ],
    )(ocols, ocnt, pcols, pcnt, edge, pt, got_off, own1)
    got_ron2 = lax.ppermute(ron2, AXES, on_pairs)

    return call(final_kernel, [VMEM] * 3, VMEM, shape((2, CP, BAND * CP)), [])(own2, got_roff, got_ron2)


def solution(mesh):
    placed = (
        P(AXES, None, None, None),
        P(AXES, None),
        P(AXES),
        P(AXES, None, None, None),
        P(AXES, None),
        P(AXES),
    )
    return jax.shard_map(
        on_device, mesh=mesh, in_specs=placed, out_specs=P(AXES, None, None), check_vma=False
    )
```

```python
import jax
import jax.numpy as jnp
from jax import lax
from jax.experimental import pallas as pl
from jax.experimental.pallas import tpu as pltpu
from jax.sharding import PartitionSpec as P

AXES = ("row", "grp")
PANEL = 256
CP = 128
HALF = 4
SLOTS = 3
BAND = 11
DEAD = 7
TILE3 = SLOTS * CP
PAY = HALF * TILE3
META = 16
VMEM_LIMIT = 45 * 1024 * 1024
UNROLL = 12
PCOLS, OCNT, PCNT = 8, 11, 12
F32 = jnp.float32
BF16 = jnp.bfloat16


def device_id():
    grp = lax.axis_index("grp")
    return lax.axis_index("row") * lax.axis_size("grp") + grp, lax.rem(grp, 2)


def slot_of(table, device, panel, slot):
    s = table[PCOLS + slot, panel] - (2 * device + lax.div(panel, HALF)) + 2
    return jnp.where(slot < table[PCNT, panel], s, DEAD)


def rows_at(ref, start, size, step=CP):
    return ref[pl.ds(pl.multiple_of(start, step), size), :]


def dot(a, b):
    return jnp.dot(a, b, preferred_element_type=F32)


def dot_nt(a, b):
    return lax.dot_general(a, b, (((1,), (1,)), ((), ())), preferred_element_type=F32)


def off_hits(table, device, parity, hits):
    found = 0
    for il in range(HALF):
        i = parity * HALF + il
        live = table[OCNT, i]
        columns = [table[i, k] for k in range(1, 8)]
        for k, j in enumerate(columns, 1):
            jo = j - 8 * device + jnp.where(parity == 1, -8, HALF)
            hits[found] = il * 64 + k * 8 + jo
            found += ((k < live) & (jo >= 0) & (jo < HALF)).astype(jnp.int32)
    return found


def field(code, shift, bits):
    return (code >> shift) & (2**bits - 1)


def clear(ref, count):
    @pl.loop(0, count)
    def _(n):
        ref[n] = jnp.zeros(ref.shape[1:], F32)


def first_kernel(table, oper, tiles, pt, out, abuf, raw, acc, hits, sems, asem):
    device, parity = device_id()
    copies = [
        pltpu.make_async_copy(tiles.at[pl.ds(half * HALF * SLOTS, HALF * SLOTS)], raw.at[at], sems.at[at])
        for at, half in enumerate((parity, 1 - parity))
    ]
    for copy in copies:
        copy.start()
    count = off_hits(table, device, parity, hits)

    def a_copy(n):
        code = hits[n]
        return pltpu.make_async_copy(
            oper.at[parity * HALF + field(code, 6, 2), field(code, 3, 3)], abuf.at[n], asem.at[n]
        )

    @pl.loop(0, count)
    def _(n):
        a_copy(n).start()

    lane = lax.broadcasted_iota(jnp.int32, (META, PANEL), 1)
    for ref, at, half in ((out, PAY, parity), (pt, 2 * PAY, 1 - parity)):
        values = jnp.zeros((META, PANEL), jnp.int32)
        for p in range(HALF):
            for t in range(SLOTS):
                s = slot_of(table, device, half * HALF + p, t)
                values = jnp.where(lane == p * SLOTS + t, s, values)
        ref[at : at + META, :] = values.astype(F32).astype(BF16)
    for n in range(2 * HALF):
        acc[n] = jnp.zeros((CP, PANEL), F32)
    for at, half in enumerate((parity, 1 - parity)):
        copies[at].wait()
        for n in range(HALF * SLOTS):
            turned = raw[at, n].T
            pt[pl.ds(pl.multiple_of(half * PAY + n * CP, CP), CP), :] = turned
            if at == 0:
                out[n * CP : (n + 1) * CP, :] = turned

    @pl.loop(0, count)
    def _(n):
        a_copy(n).wait()

    @pl.loop(0, lax.div(count + 3, 4))
    def _(block):
        for u in range(4):
            n = block * 4 + u
            code = hits[n]
            il, jo = field(code, 6, 2), field(code, 0, 2)
            res = dot(rows_at(out, (il * SLOTS + 1) * CP, 2 * CP), abuf[n])
            for t in range(1, SLOTS):
                s = slot_of(table, device, parity * HALF + il, t)
                near = s == jnp.where(parity == 1, 3, 1)
                far = s == jnp.where(parity == 1, 4, 0)
                at = jnp.where(near, jo * 2, jnp.where(far, jo * 2 + 1, 8))
                acc[jnp.where(n < count, at, 8)] += res[(t - 1) * CP : t * CP]

    for n in range(2 * HALF):
        out[PAY + META + n * CP : PAY + META + (n + 1) * CP, :] = acc[n].astype(BF16)


def local_kernel(
    table, oper, pt, got, roff, ron_near, ron_far, own, abuf, px, prod, acc, vec, smem, slots, hits, asem, psem
):
    device, parity = device_id()
    on = 1 - parity
    vec[...] = got[2 * PAY :, :CP].astype(F32).astype(jnp.int32)[:1]
    meta = pltpu.make_async_copy(vec, smem, psem.at[2])
    copies = [
        pltpu.make_async_copy(pt.at[pl.ds(0, 2 * PAY)], px.at[pl.ds(0, 2 * PAY)], psem.at[0]),
        pltpu.make_async_copy(
            got.at[pl.ds(pl.multiple_of(parity * PAY, PAY), PAY)], px.at[pl.ds(2 * PAY, PAY)], psem.at[1]
        ),
    ]
    meta.start()
    for copy in copies:
        copy.start()

    def a_copy(n):
        code = hits[n]
        return pltpu.make_async_copy(oper.at[field(code, 9, 3), field(code, 6, 3)], abuf.at[n], asem.at[n])

    count = 0
    for i in range(8):
        began = count
        live = table[OCNT, i]
        columns = [table[i, k] for k in range(8)]
        for k, column in enumerate(columns):
            j = column - 8 * device
            mine = (j >= 0) & (j < 8)
            jn = j + jnp.where(parity == 1, HALF, -8)
            theirs = (jn >= 0) & (jn < HALF)
            x = jnp.where(mine, j, 8 + jn)
            base = ((j + 8) >> 2) - 1 - i // HALF
            hits[count] = i * 512 + k * 64 + x * 4 + base
            count += ((k < live) & (mine | theirs)).astype(jnp.int32)

        @pl.loop(began, count)
        def _(n):
            a_copy(n).start()

    for t in range(SLOTS):
        own_slots = [slot_of(table, device, i, t) for i in range(8)]
        for i in range(8):
            slots[i * SLOTS + t] = own_slots[i]
    clear(prod, 64)
    clear(acc, 48)
    meta.wait()
    their_slots = [smem[0, n] for n in range(HALF * SLOTS)]
    for n in range(HALF * SLOTS):
        slots[8 * SLOTS + n] = their_slots[n]
    for copy in copies:
        copy.wait()

    @pl.loop(0, lax.div(count + UNROLL - 1, UNROLL))
    def _(block):
        @pl.loop(block * UNROLL, jnp.minimum(block * UNROLL + UNROLL, count))
        def _(n):
            a_copy(n).wait()

        for u in range(UNROLL):
            n = jnp.minimum(block * UNROLL + u, count - 1)
            code = hits[n]
            i, x, base = field(code, 9, 3), field(code, 2, 4), field(code, 0, 2)
            base = jnp.where(block * UNROLL + u < count, i * 8 + base, 64)
            res = dot_nt(rows_at(px, x * TILE3, TILE3), abuf[n])
            for t in range(SLOTS):
                s = slots[x * SLOTS + t]
                prod[jnp.where(s < DEAD, base + s, 64)] += res[t * CP : (t + 1) * CP]

    @pl.loop(0, 2)
    def _(m):
        for p in range(HALF):
            i = m * HALF + p
            lhs = rows_at(px, i * TILE3, TILE3)
            at = []
            for t in range(SLOTS):
                s = slots[i * SLOTS + t]
                at.append(jnp.where(s < DEAD, m + s, 6) * 8 + m)
            for q0 in range(0, 7, 2):
                wide = min(2, 7 - q0)
                rhs = jnp.concatenate([prod[i * 8 + q0 + w].astype(BF16) for w in range(wide)], axis=0)
                res = dot_nt(lhs, rhs)
                for t in range(SLOTS):
                    for w in range(wide):
                        acc[at[t] + q0 + w] += res[t * CP : (t + 1) * CP, w * CP : (w + 1) * CP]

    near = jnp.where(parity == 1, 4, 1)
    far = jnp.where(parity == 1, 5, 0)
    for p in range(7):
        roff[p] = acc[near * 8 + p + on].astype(BF16)
    for p in range(6):
        roff[7 + p] = acc[far * 8 + p + 1].astype(BF16)
    near = jnp.where(parity == 1, 1, 4)
    far = jnp.where(parity == 1, 0, 5)
    for p in range(8):
        ron_near[p] = acc[near * 8 + p].astype(BF16)
    for p in range(7):
        ron_far[p] = acc[far * 8 + p + on].astype(BF16)
    for r in range(2):
        for b in range(BAND):
            cb = b - 2 + r
            if 0 <= cb < 8:
                own[r * BAND + b] = acc[(r + 2) * 8 + cb]
            else:
                own[r * BAND + b] = jnp.zeros((CP, CP), F32)


def remote_kernel(
    table, abuf, pt, pay, own1, own, ron, prod, acc, vec, smem, slots, hits, psem
):
    device, parity = device_id()
    vec[...] = pay[PAY : PAY + META, :CP].astype(F32).astype(jnp.int32)[:1]
    meta = pltpu.make_async_copy(vec, smem, psem.at[0])
    meta.start()
    count = off_hits(table, device, parity, hits)
    for il in range(HALF):
        for t in range(SLOTS):
            slots[il * SLOTS + t] = slot_of(table, device, parity * HALF + il, t)
    clear(prod, HALF * 6)
    for n in range(22):
        acc[n] = own1[n]
    for n in range(22, 27):
        acc[n] = jnp.zeros((CP, CP), F32)
    meta.wait()

    @pl.loop(0, lax.div(count + 3, 4))
    def _(block):
        for u in range(4):
            n = jnp.minimum(block * 4 + u, count - 1)
            code = hits[n]
            il, jo = field(code, 6, 2), field(code, 0, 2)
            res = dot_nt(rows_at(pay, jo * TILE3, TILE3), abuf[n])
            for t in range(SLOTS):
                s = smem[0, jo * SLOTS + t]
                live = (s < DEAD) & (block * 4 + u < count)
                prod[jnp.where(live, il * 6 + s, 5)] += res[t * CP : (t + 1) * CP]

    on_row = jnp.where(parity == 1, -1, 2)
    shift = jnp.where(parity == 1, 5, 2)
    for il in range(HALF):
        lhs = rows_at(pt, (parity * HALF + il) * TILE3, TILE3)
        b_at = PAY + META + il * 2 * CP
        b_res = dot_nt(pay[b_at : b_at + 2 * CP, :], lhs)
        at = []
        for t in range(SLOTS):
            s = slots[il * SLOTS + t]
            r = parity + s - 2
            mine = (r >= 0) & (r < 2)
            base = jnp.where(mine, r * BAND + shift - r, jnp.where(r == on_row, 22, 27))
            at.append(jnp.where(s < DEAD, base, 27))
            for near in range(2):
                r = parity if near == 0 else 1 - parity
                b_row = jnp.where(s < DEAD, r * BAND + parity + s + 3 - r, 27)
                acc[b_row] += b_res[near * CP : (near + 1) * CP, t * CP : (t + 1) * CP]
        for q0 in range(0, 5, 2):
            wide = min(2, 5 - q0)
            rhs = jnp.concatenate([prod[il * 6 + q0 + w].astype(BF16) for w in range(wide)], axis=0)
            res = dot_nt(lhs, rhs)
            for t in range(SLOTS):
                for w in range(wide):
                    acc[at[t] + q0 + w] += res[t * CP : (t + 1) * CP, w * CP : (w + 1) * CP]

    for n in range(22):
        own[n] = acc[n]
    for n in range(5):
        ron[n] = acc[22 + n].astype(BF16)


def final_kernel(own, roff, near, far, ron, out):
    _, parity = device_id()
    on = 1 - parity
    for r in range(2):
        for b in range(BAND):
            out[r, :, b * CP : (b + 1) * CP] = own[r * BAND + b]

    def add(r, b, value):
        cols = pl.ds(pl.multiple_of(b * CP, CP), CP)
        out[r, :, cols] += value

    for p in range(7):
        add(parity, p + 4 * parity, roff[p].astype(F32))
    for p in range(6):
        add(on, p + 5 * parity, roff[7 + p].astype(F32))
    for p in range(5):
        add(on, p + 6 * on, ron[p].astype(F32))
    for p in range(8):
        add(on, p + 3 * on, near[p].astype(F32))
    for p in range(7):
        add(parity, p + 4 * on, far[p].astype(F32))


ANY = pl.BlockSpec(memory_space=pl.ANY)
HBM = pl.BlockSpec(memory_space=pltpu.HBM)
VMEM = pl.BlockSpec(memory_space=pltpu.VMEM)
SMEM = pl.BlockSpec(memory_space=pltpu.SMEM)


def call(kernel, in_specs, out_specs, out_shape, scratch):
    return pl.pallas_call(
        kernel,
        in_specs=in_specs,
        out_specs=out_specs,
        out_shape=out_shape,
        scratch_shapes=scratch,
        compiler_params=pltpu.CompilerParams(vmem_limit_bytes=VMEM_LIMIT),
        cost_estimate=pl.CostEstimate(flops=1000, bytes_accessed=1000, transcendentals=0),
    )


def shape(dims, dtype=F32):
    return jax.ShapeDtypeStruct(dims, dtype)


def on_device(oper, ocols, ocnt, ptiles, pcols, pcnt):
    size = lax.axis_size(AXES)
    on_pairs = [(i, i ^ 1) for i in range(size)]
    off_pairs = [(i, i + 1) for i in range(1, size - 1, 2)]
    off_pairs += [(j, i) for i, j in off_pairs]
    tiles = ptiles.reshape(8 * SLOTS, PANEL, CP)
    dma = pltpu.SemaphoreType.DMA
    i32 = jnp.int32
    meta = [pltpu.VMEM((1, CP), i32), pltpu.SMEM((1, CP), i32), pltpu.SMEM((64,), i32)]

    table = jnp.concatenate([ocols, pcols.T, ocnt[None], pcnt[None]])
    pt, pay_off, edge = call(
        first_kernel,
        [SMEM, HBM, HBM],
        [VMEM] * 3,
        [
            shape((2 * PAY + META, PANEL), BF16),
            shape((PAY + META + 8 * CP, PANEL), BF16),
            shape((12, PANEL, PANEL), BF16),
        ],
        [
            pltpu.VMEM((2, HALF * SLOTS, PANEL, CP), BF16),
            pltpu.VMEM((9, CP, PANEL), F32),
            pltpu.SMEM((32,), i32),
            dma((2,)),
            dma((12,)),
        ],
    )(table, oper, tiles)
    got_on = lax.ppermute(pt, AXES, on_pairs)
    got_off = lax.ppermute(pay_off, AXES, off_pairs)

    roff, near, far, own1 = call(
        local_kernel,
        [SMEM, HBM, VMEM, VMEM],
        [VMEM] * 4,
        [shape((13, CP, CP), BF16), shape((8, CP, CP), BF16), shape((7, CP, CP), BF16), shape((22, CP, CP))],
        [
            pltpu.VMEM((64, PANEL, PANEL), BF16),
            pltpu.VMEM((3 * PAY, PANEL), BF16),
            pltpu.VMEM((72, CP, PANEL), F32),
            pltpu.VMEM((56, CP, CP), F32),
            *meta,
            pltpu.SMEM((72,), i32),
            dma((64,)),
            dma((3,)),
        ],
    )(table, oper, pt, got_on)
    got_roff = lax.ppermute(roff, AXES, off_pairs)
    got_near = lax.ppermute(near, AXES, on_pairs)
    got_far = lax.ppermute(far, AXES, on_pairs)

    own2, ron2 = call(
        remote_kernel,
        [SMEM] + [VMEM] * 4,
        [VMEM] * 2,
        [shape((22, CP, CP)), shape((5, CP, CP), BF16)],
        [
            pltpu.VMEM((HALF * 6, CP, PANEL), F32),
            pltpu.VMEM((32, CP, CP), F32),
            *meta,
            pltpu.SMEM((32,), i32),
            dma((1,)),
        ],
    )(table, edge, pt, got_off, own1)
    got_ron2 = lax.ppermute(ron2, AXES, on_pairs)

    return call(final_kernel, [VMEM] * 5, VMEM, shape((2, CP, BAND * CP)), [])(
        own2, got_roff, got_near, got_far, got_ron2
    )


def solution(mesh):
    placed = (
        P(AXES, None, None, None),
        P(AXES, None),
        P(AXES),
        P(AXES, None, None, None),
        P(AXES, None),
        P(AXES),
    )
    return jax.shard_map(
        on_device, mesh=mesh, in_specs=placed, out_specs=P(AXES, None, None), check_vma=False
    )
```

```python
import jax
import jax.numpy as jnp
from jax import lax
from jax.experimental import pallas as pl
from jax.experimental.pallas import tpu as pltpu
from jax.sharding import PartitionSpec as P

AXES = ("row", "grp")
PANEL = 256
CP = 128
HALF = 4
SLOTS = 3
BAND = 11
DEAD = 7
TILE3 = SLOTS * CP
PAY = HALF * TILE3
META = 16
VMEM_LIMIT = 45 * 1024 * 1024
UNROLL = 12
PCOLS, OCNT, PCNT = 8, 11, 12
F32 = jnp.float32
BF16 = jnp.bfloat16


def device_id():
    grp = lax.axis_index("grp")
    return lax.axis_index("row") * lax.axis_size("grp") + grp, lax.rem(grp, 2)


def slot_of(table, device, panel, slot):
    s = table[PCOLS + slot, panel] - (2 * device + lax.div(panel, HALF)) + 2
    return jnp.where(slot < table[PCNT, panel], s, DEAD)


def rows_at(ref, start, size, step=CP):
    return ref[pl.ds(pl.multiple_of(start, step), size), :]


def dot(a, b):
    return jnp.dot(a, b, preferred_element_type=F32)


def dot_nt(a, b):
    return lax.dot_general(a, b, (((1,), (1,)), ((), ())), preferred_element_type=F32)


def off_hits(table, device, parity, hits):
    found = 0
    for il in range(HALF):
        i = parity * HALF + il
        live = table[OCNT, i]
        columns = [table[i, k] for k in range(1, 8)]
        for k, j in enumerate(columns, 1):
            jo = j - 8 * device + jnp.where(parity == 1, -8, HALF)
            hits[found] = il * 64 + k * 8 + jo
            found += ((k < live) & (jo >= 0) & (jo < HALF)).astype(jnp.int32)
    return found


def field(code, shift, bits):
    return (code >> shift) & (2**bits - 1)


def clear(ref, count):
    @pl.loop(0, count)
    def _(n):
        ref[n] = jnp.zeros(ref.shape[1:], F32)


def first_kernel(table, oper, tiles, pt, out, abuf, raw, acc, hits, sems, asem):
    device, parity = device_id()
    copies = [
        pltpu.make_async_copy(tiles.at[pl.ds(half * HALF * SLOTS, HALF * SLOTS)], raw.at[at], sems.at[at])
        for at, half in enumerate((parity, 1 - parity))
    ]
    for copy in copies:
        copy.start()
    count = off_hits(table, device, parity, hits)

    def a_copy(n):
        code = hits[n]
        return pltpu.make_async_copy(
            oper.at[parity * HALF + field(code, 6, 2), field(code, 3, 3)], abuf.at[n], asem.at[n]
        )

    @pl.loop(0, count)
    def _(n):
        a_copy(n).start()

    lane = lax.broadcasted_iota(jnp.int32, (META, PANEL), 1)
    for ref, at, half in ((out, PAY, parity), (pt, 2 * PAY, 1 - parity)):
        values = jnp.zeros((META, PANEL), jnp.int32)
        for p in range(HALF):
            for t in range(SLOTS):
                s = slot_of(table, device, half * HALF + p, t)
                values = jnp.where(lane == p * SLOTS + t, s, values)
        ref[at : at + META, :] = values.astype(F32).astype(BF16)
    for n in range(2 * HALF):
        acc[n] = jnp.zeros((CP, PANEL), F32)
    for at, half in enumerate((parity, 1 - parity)):
        copies[at].wait()
        for n in range(HALF * SLOTS):
            turned = raw[at, n].T
            pt[pl.ds(pl.multiple_of(half * PAY + n * CP, CP), CP), :] = turned
            if at == 0:
                out[n * CP : (n + 1) * CP, :] = turned

    @pl.loop(0, count)
    def _(n):
        a_copy(n).wait()

    @pl.loop(0, lax.div(count + 3, 4))
    def _(block):
        for u in range(4):
            n = block * 4 + u
            code = hits[n]
            il, jo = field(code, 6, 2), field(code, 0, 2)
            res = dot(rows_at(out, (il * SLOTS + 1) * CP, 2 * CP), abuf[n])
            for t in range(1, SLOTS):
                s = slot_of(table, device, parity * HALF + il, t)
                near = s == jnp.where(parity == 1, 3, 1)
                far = s == jnp.where(parity == 1, 4, 0)
                at = jnp.where(near, jo * 2, jnp.where(far, jo * 2 + 1, 8))
                acc[jnp.where(n < count, at, 8)] += res[(t - 1) * CP : t * CP]

    for n in range(2 * HALF):
        out[PAY + META + n * CP : PAY + META + (n + 1) * CP, :] = acc[n].astype(BF16)


def local_kernel(
    table, oper, pt, got, roff, ron_near, ron_far, own, abuf, px, prod, acc, vec, smem, slots, hits, asem, psem
):
    device, parity = device_id()
    on = 1 - parity
    vec[...] = got[2 * PAY :, :CP].astype(F32).astype(jnp.int32)[:1]
    meta = pltpu.make_async_copy(vec, smem, psem.at[2])
    copies = [
        pltpu.make_async_copy(pt.at[pl.ds(0, 2 * PAY)], px.at[pl.ds(0, 2 * PAY)], psem.at[0]),
        pltpu.make_async_copy(
            got.at[pl.ds(pl.multiple_of(parity * PAY, PAY), PAY)], px.at[pl.ds(2 * PAY, PAY)], psem.at[1]
        ),
    ]
    meta.start()
    for copy in copies:
        copy.start()

    def a_copy(n):
        code = hits[n]
        return pltpu.make_async_copy(oper.at[field(code, 9, 3), field(code, 6, 3)], abuf.at[n], asem.at[n])

    count = 0
    for i in range(8):
        began = count
        live = table[OCNT, i]
        columns = [table[i, k] for k in range(8)]
        for k, column in enumerate(columns):
            j = column - 8 * device
            mine = (j >= 0) & (j < 8)
            jn = j + jnp.where(parity == 1, HALF, -8)
            theirs = (jn >= 0) & (jn < HALF)
            x = jnp.where(mine, j, 8 + jn)
            base = ((j + 8) >> 2) - 1 - i // HALF
            hits[count] = i * 512 + k * 64 + x * 4 + base
            count += ((k < live) & (mine | theirs)).astype(jnp.int32)

        @pl.loop(began, count)
        def _(n):
            a_copy(n).start()

    for t in range(SLOTS):
        own_slots = [slot_of(table, device, i, t) for i in range(8)]
        for i in range(8):
            slots[i * SLOTS + t] = own_slots[i]
    clear(prod, 64)
    clear(acc, 48)
    meta.wait()
    their_slots = [smem[0, n] for n in range(HALF * SLOTS)]
    for n in range(HALF * SLOTS):
        slots[8 * SLOTS + n] = their_slots[n]
    for copy in copies:
        copy.wait()

    @pl.loop(0, lax.div(count + UNROLL - 1, UNROLL))
    def _(block):
        @pl.loop(block * UNROLL, jnp.minimum(block * UNROLL + UNROLL, count))
        def _(n):
            a_copy(n).wait()

        for u in range(UNROLL):
            n = jnp.minimum(block * UNROLL + u, count - 1)
            code = hits[n]
            i, x, base = field(code, 9, 3), field(code, 2, 4), field(code, 0, 2)
            base = jnp.where(block * UNROLL + u < count, i * 8 + base, 64)
            res = dot_nt(rows_at(px, x * TILE3, TILE3), abuf[n])
            for t in range(SLOTS):
                s = slots[x * SLOTS + t]
                prod[jnp.where(s < DEAD, base + s, 64)] += res[t * CP : (t + 1) * CP]

    for m in range(2):
        for p in range(HALF):
            i = m * HALF + p
            lhs = rows_at(px, i * TILE3, TILE3)
            at = []
            for t in range(SLOTS):
                s = slots[i * SLOTS + t]
                at.append(jnp.where(s < DEAD, m + s, 6) * 8 + m)
            for q0 in range(0, 7, 2):
                wide = min(2, 7 - q0)
                rhs = jnp.concatenate([prod[i * 8 + q0 + w].astype(BF16) for w in range(wide)], axis=0)
                res = dot_nt(lhs, rhs)
                for t in range(SLOTS):
                    for w in range(wide):
                        acc[at[t] + q0 + w] += res[t * CP : (t + 1) * CP, w * CP : (w + 1) * CP]

    near = jnp.where(parity == 1, 4, 1)
    far = jnp.where(parity == 1, 5, 0)
    for p in range(7):
        roff[p] = acc[near * 8 + p + on].astype(BF16)
    for p in range(6):
        roff[7 + p] = acc[far * 8 + p + 1].astype(BF16)
    near = jnp.where(parity == 1, 1, 4)
    far = jnp.where(parity == 1, 0, 5)
    for p in range(8):
        ron_near[p] = acc[near * 8 + p].astype(BF16)
    for p in range(7):
        ron_far[p] = acc[far * 8 + p + on].astype(BF16)
    for r in range(2):
        for b in range(BAND):
            cb = b - 2 + r
            if 0 <= cb < 8:
                own[r * BAND + b] = acc[(r + 2) * 8 + cb]
            else:
                own[r * BAND + b] = jnp.zeros((CP, CP), F32)


def remote_kernel(
    table, abuf, pt, pay, own1, own, ron, prod, acc, vec, smem, slots, hits, psem
):
    device, parity = device_id()
    vec[...] = pay[PAY : PAY + META, :CP].astype(F32).astype(jnp.int32)[:1]
    meta = pltpu.make_async_copy(vec, smem, psem.at[0])
    meta.start()
    count = off_hits(table, device, parity, hits)
    for il in range(HALF):
        for t in range(SLOTS):
            slots[il * SLOTS + t] = slot_of(table, device, parity * HALF + il, t)
    clear(prod, HALF * 6)
    for n in range(22):
        acc[n] = own1[n]
    for n in range(22, 27):
        acc[n] = jnp.zeros((CP, CP), F32)
    meta.wait()

    @pl.loop(0, lax.div(count + 3, 4))
    def _(block):
        for u in range(4):
            n = jnp.minimum(block * 4 + u, count - 1)
            code = hits[n]
            il, jo = field(code, 6, 2), field(code, 0, 2)
            res = dot_nt(rows_at(pay, jo * TILE3, TILE3), abuf[n])
            for t in range(SLOTS):
                s = smem[0, jo * SLOTS + t]
                live = (s < DEAD) & (block * 4 + u < count)
                prod[jnp.where(live, il * 6 + s, 5)] += res[t * CP : (t + 1) * CP]

    on_row = jnp.where(parity == 1, -1, 2)
    shift = jnp.where(parity == 1, 5, 2)
    for il in range(HALF):
        lhs = rows_at(pt, (parity * HALF + il) * TILE3, TILE3)
        b_at = PAY + META + il * 2 * CP
        b_res = dot_nt(pay[b_at : b_at + 2 * CP, :], lhs)
        at = []
        for t in range(SLOTS):
            s = slots[il * SLOTS + t]
            r = parity + s - 2
            mine = (r >= 0) & (r < 2)
            base = jnp.where(mine, r * BAND + shift - r, jnp.where(r == on_row, 22, 27))
            at.append(jnp.where(s < DEAD, base, 27))
            for near in range(2):
                r = parity if near == 0 else 1 - parity
                b_row = jnp.where(s < DEAD, r * BAND + parity + s + 3 - r, 27)
                acc[b_row] += b_res[near * CP : (near + 1) * CP, t * CP : (t + 1) * CP]
        for q0 in range(0, 5, 2):
            wide = min(2, 5 - q0)
            rhs = jnp.concatenate([prod[il * 6 + q0 + w].astype(BF16) for w in range(wide)], axis=0)
            res = dot_nt(lhs, rhs)
            for t in range(SLOTS):
                for w in range(wide):
                    acc[at[t] + q0 + w] += res[t * CP : (t + 1) * CP, w * CP : (w + 1) * CP]

    for n in range(22):
        own[n] = acc[n]
    for n in range(5):
        ron[n] = acc[22 + n].astype(BF16)


def final_kernel(own, roff, near, far, ron, out):
    _, parity = device_id()
    on = 1 - parity
    for r in range(2):
        for b in range(BAND):
            out[r, :, b * CP : (b + 1) * CP] = own[r * BAND + b]

    def add(r, b, value):
        cols = pl.ds(pl.multiple_of(b * CP, CP), CP)
        out[r, :, cols] += value

    for p in range(7):
        add(parity, p + 4 * parity, roff[p].astype(F32))
    for p in range(6):
        add(on, p + 5 * parity, roff[7 + p].astype(F32))
    for p in range(5):
        add(on, p + 6 * on, ron[p].astype(F32))
    for p in range(8):
        add(on, p + 3 * on, near[p].astype(F32))
    for p in range(7):
        add(parity, p + 4 * on, far[p].astype(F32))


ANY = pl.BlockSpec(memory_space=pl.ANY)
HBM = pl.BlockSpec(memory_space=pltpu.HBM)
VMEM = pl.BlockSpec(memory_space=pltpu.VMEM)
SMEM = pl.BlockSpec(memory_space=pltpu.SMEM)


def call(kernel, in_specs, out_specs, out_shape, scratch):
    return pl.pallas_call(
        kernel,
        in_specs=in_specs,
        out_specs=out_specs,
        out_shape=out_shape,
        scratch_shapes=scratch,
        compiler_params=pltpu.CompilerParams(vmem_limit_bytes=VMEM_LIMIT),
        cost_estimate=pl.CostEstimate(flops=1000, bytes_accessed=1000, transcendentals=0),
    )


def shape(dims, dtype=F32):
    return jax.ShapeDtypeStruct(dims, dtype)


def on_device(oper, ocols, ocnt, ptiles, pcols, pcnt):
    size = lax.axis_size(AXES)
    on_pairs = [(i, i ^ 1) for i in range(size)]
    off_pairs = [(i, i + 1) for i in range(1, size - 1, 2)]
    off_pairs += [(j, i) for i, j in off_pairs]
    tiles = ptiles.reshape(8 * SLOTS, PANEL, CP)
    dma = pltpu.SemaphoreType.DMA
    i32 = jnp.int32
    meta = [pltpu.VMEM((1, CP), i32), pltpu.SMEM((1, CP), i32), pltpu.SMEM((64,), i32)]

    table = jnp.concatenate([ocols, pcols.T, ocnt[None], pcnt[None]])
    pt, pay_off, edge = call(
        first_kernel,
        [SMEM, HBM, HBM],
        [VMEM] * 3,
        [
            shape((2 * PAY + META, PANEL), BF16),
            shape((PAY + META + 8 * CP, PANEL), BF16),
            shape((12, PANEL, PANEL), BF16),
        ],
        [
            pltpu.VMEM((2, HALF * SLOTS, PANEL, CP), BF16),
            pltpu.VMEM((9, CP, PANEL), F32),
            pltpu.SMEM((32,), i32),
            dma((2,)),
            dma((12,)),
        ],
    )(table, oper, tiles)
    got_on = lax.ppermute(pt, AXES, on_pairs)
    got_off = lax.ppermute(pay_off, AXES, off_pairs)

    roff, near, far, own1 = call(
        local_kernel,
        [SMEM, HBM, VMEM, VMEM],
        [VMEM] * 4,
        [shape((13, CP, CP), BF16), shape((8, CP, CP), BF16), shape((7, CP, CP), BF16), shape((22, CP, CP))],
        [
            pltpu.VMEM((64, PANEL, PANEL), BF16),
            pltpu.VMEM((3 * PAY, PANEL), BF16),
            pltpu.VMEM((72, CP, PANEL), F32),
            pltpu.VMEM((56, CP, CP), F32),
            *meta,
            pltpu.SMEM((72,), i32),
            dma((64,)),
            dma((3,)),
        ],
    )(table, oper, pt, got_on)
    got_roff = lax.ppermute(roff, AXES, off_pairs)
    got_near = lax.ppermute(near, AXES, on_pairs)
    got_far = lax.ppermute(far, AXES, on_pairs)

    own2, ron2 = call(
        remote_kernel,
        [SMEM] + [VMEM] * 4,
        [VMEM] * 2,
        [shape((22, CP, CP)), shape((5, CP, CP), BF16)],
        [
            pltpu.VMEM((HALF * 6, CP, PANEL), F32),
            pltpu.VMEM((32, CP, CP), F32),
            *meta,
            pltpu.SMEM((32,), i32),
            dma((1,)),
        ],
    )(table, edge, pt, got_off, own1)
    got_ron2 = lax.ppermute(ron2, AXES, on_pairs)

    return call(final_kernel, [VMEM] * 5, VMEM, shape((2, CP, BAND * CP)), [])(
        own2, got_roff, got_near, got_far, got_ron2
    )


def solution(mesh):
    placed = (
        P(AXES, None, None, None),
        P(AXES, None),
        P(AXES),
        P(AXES, None, None, None),
        P(AXES, None),
        P(AXES),
    )
    return jax.shard_map(
        on_device, mesh=mesh, in_specs=placed, out_specs=P(AXES, None, None), check_vma=False
    )
```
